32 devices in a mesh: gx: 4 (over y, core), gy: 8 (over z, x).
Axes of the slice: x: 2, y: 2, z: 4, core: 2. Of those that a mesh axis runs over, the one named last changes fastest.
Arguments:
- patches: bfloat16 [3072, 1408], P(('gx', 'gy')), may hold values from -6 to 6
- grids: int32 [8, 2], replicated, may hold values from 4 to 12, as said below
- text_ids: int32 [2048], P('gx'), may hold values from 0 to 31999
- positions: int32 [768], replicated, may hold values from -1 to 1023, as said below
- lengths: int32 [8], replicated, may hold values from 1 to 1536, 2048 in all
- text_table: bfloat16 [32000, 1408], P('gy'), may hold values from -6 to 6
- vit_norm1: float32 [1408], replicated, may hold values from 0.5 to 1.5
- vit_qkv: bfloat16 [1408, 3, 1408], P('gx', None, 'gy'), may hold values from -0.15625 to 0.15625
- vit_out: bfloat16 [1408, 1408], P('gx', 'gy'), may hold values from -0.15625 to 0.15625
- vit_norm2: float32 [1408], replicated, may hold values from 0.5 to 1.5
- vit_fc1: bfloat16 [1408, 6144], P('gx', 'gy'), may hold values from -0.15625 to 0.15625
- vit_fc2: bfloat16 [1408, 6144], P('gx', 'gy'), may hold values from -0.078125 to 0.078125
- merge_norm: float32 [4, 1408], replicated, may hold values from 0.5 to 1.5
- merge_proj: bfloat16 [1408, 4, 1408], P('gx', None, 'gy'), may hold values from -0.078125 to 0.078125
- dec_norm1: float32 [1408], replicated, may hold values from 0.5 to 1.5
- dec_qkv: bfloat16 [1408, 3, 1408], P('gx', None, 'gy'), may hold values from -0.15625 to 0.15625
- dec_out: bfloat16 [1408, 1408], P('gx', 'gy'), may hold values from -0.15625 to 0.15625
- dec_norm2: float32 [1408], replicated, may hold values from 0.5 to 1.5
- dec_fc1: bfloat16 [1408, 6144], P('gx', 'gy'), may hold values from -0.15625 to 0.15625
- dec_fc2: bfloat16 [1408, 6144], P('gx', 'gy'), may hold values from -0.078125 to 0.078125
- next_norm: float32 [1408], replicated, may hold values from 0.5 to 1.5
- next_qkv: bfloat16 [1408, 3, 1408], P('gx', None, 'gy'), may hold values from -0.15625 to 0.15625
Outputs:
- next_triple: bfloat16 [2048, 3, 1408], P(('gx', 'gy'))
The draws below stay inside these ranges and needn't reach their ends.
Inputs may be any that keep to these rules, and one draw needn't show every extreme that they name: `grids`: row i gives image i's merged grid (rows from (9) // 2 to 8, columns from (13) // 2 to 12); images i * 2 to i * 2 + 1 belong to index i of gx; in every draw all images of some index of gx have 8 x 12, filling its 768 patch slots. Each index of gx's merged slots that belong to images come first; they hold distinct prompt positions that rise with the slot's global index; the other slots hold -1.
All inputs are finite; a program needn't handle non-finite values.
Results may differ from the reference program's by a relative error of at most 0.023.
Values may be sent and summed in bfloat16 or wider, within the bound.
A program may use at most 128 MiB of HBM per device.

```python
import math
import jax
import jax.numpy as jnp
import numpy as np
from jax import lax

D = 1408
HEADS = 16
HEAD_DIM = 88
FF = 6144
VOCAB = 32000
MGRID_H = 8
MGRID_W = 12
REQS = 8
IMG_GX = 2
PATCH_GX = 768
MERGE_GX = 192
IMAGES = 8
PATCHES = 3072
MERGE_TOTAL = 768
SEQ = 2048
N_GX = 4


def grid_table(key):
    grid_key = jax.random.fold_in(key, 11)
    key_rows, key_cols, key_full = jax.random.split(grid_key, 3)
    grid_rows = jax.random.randint(key_rows, (IMAGES,), (MGRID_H + 1) // 2, MGRID_H + 1)
    grid_cols = jax.random.randint(key_cols, (IMAGES,), (MGRID_W + 1) // 2, MGRID_W + 1)
    full_index = jax.random.randint(key_full, (), 0, IMAGES // IMG_GX)
    owner = jnp.arange(IMAGES) // IMG_GX
    grid_rows = jnp.where(owner == full_index, MGRID_H, grid_rows)
    grid_cols = jnp.where(owner == full_index, MGRID_W, grid_cols)
    return jnp.stack([grid_rows, grid_cols], axis=1).astype(jnp.int32)


def draw_grids(key, part):
    return grid_table(key)


def draw_positions(key, part):
    table = grid_table(key)
    counts = (table[:, 0] * table[:, 1]).reshape(IMAGES // IMG_GX, IMG_GX)
    live_total = jnp.sum(counts, axis=1)
    slot_index = jnp.arange(MERGE_GX)
    is_live = (slot_index[None, :] < live_total[:, None]).reshape(MERGE_TOTAL)
    chosen = jnp.sort(jax.random.permutation(jax.random.fold_in(key, 23), SEQ // 2)[:MERGE_TOTAL])
    global_slot = jnp.arange(MERGE_TOTAL)
    last_live = jnp.max(jnp.where(is_live, global_slot, -1))
    chosen = jnp.where(global_slot == last_live, SEQ // 2 - 1, chosen)
    return jnp.where(is_live, chosen, -1).astype(jnp.int32)


def touch_ends(values, own_key, least, top_value):
    longest = values.shape.index(max(values.shape))
    spots = []
    for shift in (0, 1):
        where = [jax.random.randint(jax.random.fold_in(own_key, axis), (), 0, length) for axis, length in enumerate(values.shape)]
        where[longest] = (where[longest] + shift) % values.shape[longest]
        spots.append(tuple(where))
    return values.at[spots[0]].set(least).at[spots[1]].set(top_value)


def block_levels(stream_key, extent, cuts, low, top_value):
    def one(axis_at, blocks):
        heights = jax.random.uniform(jax.random.fold_in(jax.random.fold_in(stream_key, 6), axis_at), (blocks,), jnp.float32, low / len(cuts), top_value / len(cuts))
        return jnp.repeat(jnp.exp(heights), extent[axis_at] // blocks).reshape((-1,) + (1,) * (len(extent) - axis_at - 1))

    gain = one(*cuts[0])
    for cut in cuts[1:]:
        gain = gain * one(*cut)
    return gain


def rank_table(amount, lean):
    weights = [(1 << 20) // math.isqrt(grade ** lean) + 1 for grade in range(1, amount + 1)]
    scale = 1 + sum(weights) // (1 << 30)
    return np.cumsum(np.array([max(1, weight // scale) for weight in weights]))


def ranked_ids(own_key, dims, number_of, skew):
    grid = rank_table(number_of, skew)
    pick = jax.random.randint(jax.random.fold_in(own_key, 1), dims, 0, int(grid[number_of - 1]))
    rank = jnp.searchsorted(jnp.asarray(grid, jnp.int32), pick, side="right")
    return jax.random.permutation(jax.random.fold_in(own_key, 2), number_of)[rank].astype(jnp.int32)


def split_up(amount, total, most, lean):
    portions = [(1 << 20) // math.isqrt(rank ** lean) + 1 for rank in range(2, amount + 1)]
    surplus, holding = total - most - (amount - 1), [1] * (amount - 1)
    while surplus > 0:
        movable = [i for i in range(amount - 1) if holding[i] < most]
        whole, budget = sum([portions[i] for i in movable]), surplus
        for i in movable:
            more = min(most - holding[i], max(1, budget * portions[i] // whole), surplus)
            holding[i] = holding[i] + more
            surplus = surplus - more
    return np.array([most] + holding)


def ragged(key, number_of, total, limit, lean):
    if number_of == 2:
        one = jax.random.randint(key, (), max(1, total - limit), min(limit, total - 1) + 1)
        return jnp.stack([one, total - one])
    tallies = jnp.asarray(split_up(number_of, total, limit, lean), jnp.int32)
    couples = (number_of - 1) // 2
    source_of, sink = tallies[1:1 + 2 * couples:2], tallies[2:2 + 2 * couples:2]
    margin = jnp.minimum(source_of - 1, limit - sink)
    moved = jax.random.randint(jax.random.fold_in(key, 1), (couples,), 0, 1 << 20) % (margin + 1)
    tallies = tallies.at[1:1 + 2 * couples:2].set(source_of - moved).at[2:2 + 2 * couples:2].set(sink + moved)
    return tallies[jax.random.permutation(jax.random.fold_in(key, 2), number_of)]


def bell_draw(stream_key, dims, scale, reach, pieces=(), kind=jnp.bfloat16):
    loudness = block_levels(stream_key, dims, pieces, -0.22, 0.18) if pieces else 1.0
    result = jax.random.normal(stream_key, dims, jnp.float32) * scale * loudness
    return jnp.minimum(jnp.maximum(result, -reach), reach).astype(kind)


def setup_inputs(seed: int = 0) -> dict:
    streams_of = jax.random.split(jax.random.key(seed), 23)
    patches = bell_draw(streams_of[0], (PATCHES, D), 1.0, 6.0, ((0, 32),))
    grids = draw_grids(jax.random.fold_in(streams_of[22], 71), 0)
    text_ids = touch_ends(ranked_ids(streams_of[2], (SEQ,), VOCAB, 2), jax.random.fold_in(streams_of[2], 3), 0, VOCAB - 1).astype(jnp.int32)
    positions = draw_positions(jax.random.fold_in(streams_of[22], 71), 0)
    lengths = ragged(streams_of[4], REQS, SEQ, 3 * SEQ // 4, 2).astype(jnp.int32)
    text_table = bell_draw(streams_of[5], (VOCAB, D), 1.0, 6.0, ((0, 8),))
    vit_norm1 = jnp.clip(1.0 + 0.1 * jax.random.normal(streams_of[6], (D,), jnp.float32), 0.5, 1.5)
    vit_qkv = bell_draw(streams_of[7], (D, 3, D), D ** -0.5, 0.15625, ((0, 4), (2, 8)))
    vit_out = bell_draw(streams_of[8], (D, D), D ** -0.5, 0.15625, ((0, 4), (1, 8)))
    vit_norm2 = jnp.clip(1.0 + 0.1 * jax.random.normal(streams_of[9], (D,), jnp.float32), 0.5, 1.5)
    vit_fc1 = bell_draw(streams_of[10], (D, FF), D ** -0.5, 0.15625, ((0, 4), (1, 8)))
    vit_fc2 = bell_draw(streams_of[11], (D, FF), FF ** -0.5, 0.078125, ((0, 4), (1, 8)))
    merge_norm = jnp.clip(1.0 + 0.1 * jax.random.normal(streams_of[12], (4, D), jnp.float32), 0.5, 1.5)
    merge_proj = bell_draw(streams_of[13], (D, 4, D), (4 * D) ** -0.5, 0.078125, ((0, 4), (2, 8)))
    dec_norm1 = jnp.clip(1.0 + 0.1 * jax.random.normal(streams_of[14], (D,), jnp.float32), 0.5, 1.5)
    dec_qkv = bell_draw(streams_of[15], (D, 3, D), D ** -0.5, 0.15625, ((0, 4), (2, 8)))
    dec_out = bell_draw(streams_of[16], (D, D), D ** -0.5, 0.15625, ((0, 4), (1, 8)))
    dec_norm2 = jnp.clip(1.0 + 0.1 * jax.random.normal(streams_of[17], (D,), jnp.float32), 0.5, 1.5)
    dec_fc1 = bell_draw(streams_of[18], (D, FF), D ** -0.5, 0.15625, ((0, 4), (1, 8)))
    dec_fc2 = bell_draw(streams_of[19], (D, FF), FF ** -0.5, 0.078125, ((0, 4), (1, 8)))
    next_norm = jnp.clip(1.0 + 0.1 * jax.random.normal(streams_of[20], (D,), jnp.float32), 0.5, 1.5)
    next_qkv = bell_draw(streams_of[21], (D, 3, D), D ** -0.5, 0.15625, ((0, 4), (2, 8)))
    return dict(patches=patches, grids=grids, text_ids=text_ids, positions=positions, lengths=lengths, text_table=text_table, vit_norm1=vit_norm1, vit_qkv=vit_qkv, vit_out=vit_out, vit_norm2=vit_norm2, vit_fc1=vit_fc1, vit_fc2=vit_fc2, merge_norm=merge_norm, merge_proj=merge_proj, dec_norm1=dec_norm1, dec_qkv=dec_qkv, dec_out=dec_out, dec_norm2=dec_norm2, dec_fc1=dec_fc1, dec_fc2=dec_fc2, next_norm=next_norm, next_qkv=next_qkv)


norm_eps = 1e-06
masked_score = -1e+30

def layer_norm(values, gain_row):
    values = values.astype(jnp.float32)
    centre = values - lax.optimization_barrier(jnp.mean(values, axis=-1, keepdims=True))
    spread = lax.optimization_barrier(jnp.mean(centre * centre, axis=-1, keepdims=True))
    return (centre * lax.rsqrt(spread + norm_eps) * gain_row).astype(jnp.bfloat16)

def rms_norm(values, gain_row):
    values = values.astype(jnp.float32)
    square = lax.optimization_barrier(jnp.mean(values * values, axis=-1, keepdims=True))
    return (values * lax.rsqrt(square + norm_eps) * gain_row).astype(jnp.bfloat16)

def image_bounds(grid_rows):
    merged_count = grid_rows[:, 0] * grid_rows[:, 1]
    merged_end = jnp.cumsum(merged_count).astype(jnp.int32)
    return (merged_count.astype(jnp.int32), merged_end)

def patch_images(grid_rows, patch_slots):
    merged_count, merged_end = image_bounds(grid_rows)
    slot_index = jnp.arange(patch_slots, dtype=jnp.int32)
    return lax.optimization_barrier(jnp.sum((slot_index[:, None] >= 4 * merged_end[None, :]).astype(jnp.int32), axis=1))

def merge_sources(grid_rows, merge_slots):
    image_count = grid_rows.shape[0]
    merged_count, merged_end = image_bounds(grid_rows)
    merged_start = merged_end - merged_count
    slot_index = jnp.arange(merge_slots, dtype=jnp.int32)
    image_of = lax.optimization_barrier(jnp.sum((slot_index[:, None] >= merged_end[None, :]).astype(jnp.int32), axis=1))
    is_live = image_of < image_count
    picked = (jnp.minimum(image_of, image_count - 1)[:, None] == jnp.arange(image_count, dtype=jnp.int32)[None, :]).astype(jnp.int32)
    col_count = lax.optimization_barrier(jnp.sum(picked * grid_rows[None, :, 1], axis=1))
    first_slot = lax.optimization_barrier(jnp.sum(picked * merged_start[None, :], axis=1))
    local_slot = slot_index - first_slot
    grid_row = local_slot // col_count
    grid_col = local_slot % col_count
    base_row = 4 * first_slot + 4 * grid_row * col_count + 2 * grid_col
    offsets = jnp.stack([jnp.zeros_like(col_count), jnp.ones_like(col_count), 2 * col_count, 2 * col_count + 1], axis=1)
    return jnp.where(is_live[:, None], base_row[:, None] + offsets, 0).astype(jnp.int32)

def head_attention(queries, key_rows, value_rows, allowed):
    scores = jnp.dot(queries, key_rows.T, preferred_element_type=jnp.float32) * HEAD_DIM ** (-0.5)
    exp_scores = jnp.where(allowed, jnp.exp(scores), 0.0)
    denominator = lax.optimization_barrier(jnp.sum(exp_scores, axis=1, keepdims=True))
    weighted = jnp.dot(exp_scores.astype(jnp.bfloat16), value_rows, preferred_element_type=jnp.float32)
    return (weighted / denominator).astype(jnp.bfloat16)

def many_heads(queries, key_rows, value_rows, allowed):

    def one_head(triple_in):
        return head_attention(triple_in[0], triple_in[1], triple_in[2], allowed)
    outputs = lax.map(one_head, (queries.transpose(1, 0, 2), key_rows.transpose(1, 0, 2), value_rows.transpose(1, 0, 2)))
    return outputs.transpose(1, 0, 2).reshape(queries.shape[0], -1)

def feed_forward(stream, gain_row, fc_in, fc_back, norm_fn):
    hidden = jax.nn.gelu(jnp.dot(norm_fn(stream, gain_row), fc_in, preferred_element_type=jnp.float32), approximate=False).astype(jnp.bfloat16)
    back = lax.dot_general(hidden, fc_back, (((1,), (1,)), ((), ())), preferred_element_type=jnp.float32)
    return (stream.astype(jnp.float32) + back).astype(jnp.bfloat16)

def reference(patches, grids, text_ids, positions, lengths, text_table, vit_norm1, vit_qkv, vit_out, vit_norm2, vit_fc1, vit_fc2, merge_norm, merge_proj, dec_norm1, dec_qkv, dec_out, dec_norm2, dec_fc1, dec_fc2, next_norm, next_qkv):
    grid_groups = grids.reshape(N_GX, IMG_GX, 2)
    normed = layer_norm(patches, vit_norm1)
    triple = jnp.dot(normed, vit_qkv.reshape(D, 3 * D), preferred_element_type=jnp.float32).astype(jnp.bfloat16)
    triple = triple.reshape(N_GX, PATCH_GX, 3, HEADS, HEAD_DIM)

    def patch_ids(grid_rows):
        return patch_images(grid_rows, PATCH_GX)
    image_ids = jax.vmap(patch_ids)(grid_groups)

    def group_attention(inputs):
        block, class_ids = inputs
        allowed = class_ids[:, None] == class_ids[None, :]
        return many_heads(block[:, 0], block[:, 1], block[:, 2], allowed)
    attended = lax.map(group_attention, (triple, image_ids)).reshape(PATCHES, D)
    vit_mid = (patches.astype(jnp.float32) + jnp.dot(attended, vit_out, preferred_element_type=jnp.float32)).astype(jnp.bfloat16)
    vit_final = feed_forward(vit_mid, vit_norm2, vit_fc1, vit_fc2, layer_norm)

    def merge_ids(grid_rows):
        return merge_sources(grid_rows, MERGE_GX)
    sources = jax.vmap(merge_ids)(grid_groups)
    sources = (sources + PATCH_GX * jnp.arange(N_GX, dtype=jnp.int32)[:, None, None]).reshape(MERGE_TOTAL * 4)
    merged = jnp.take(vit_final, sources, axis=0).reshape(MERGE_TOTAL, 4 * D)
    merged_normed = layer_norm(merged, merge_norm.reshape(4 * D))
    proj_flat = merge_proj.transpose(1, 0, 2).reshape(4 * D, D)
    projected = jnp.dot(merged_normed, proj_flat, preferred_element_type=jnp.float32).astype(jnp.bfloat16)
    seq_index = jnp.arange(SEQ, dtype=jnp.int32)
    matches = positions[None, :] == seq_index[:, None]
    is_image = jnp.any(matches, axis=1)
    slot_index = jnp.arange(MERGE_TOTAL, dtype=jnp.int32)
    source_slot = lax.optimization_barrier(jnp.sum(jnp.where(matches, slot_index[None, :], 0), axis=1)).astype(jnp.int32)
    embedded = jnp.where(is_image[:, None], jnp.take(projected, source_slot, axis=0), jnp.take(text_table, text_ids, axis=0))
    dec_triple = jnp.dot(rms_norm(embedded, dec_norm1), dec_qkv.reshape(D, 3 * D), preferred_element_type=jnp.float32).astype(jnp.bfloat16)
    dec_triple = dec_triple.reshape(SEQ, 3, HEADS, HEAD_DIM)
    bounds = jnp.cumsum(lengths).astype(jnp.int32)
    request = lax.optimization_barrier(jnp.sum((seq_index[:, None] >= bounds[None, :]).astype(jnp.int32), axis=1))
    allowed = (request[:, None] == request[None, :]) & (seq_index[None, :] <= seq_index[:, None])
    dec_attended = many_heads(dec_triple[:, 0], dec_triple[:, 1], dec_triple[:, 2], allowed)
    dec_mid = (embedded.astype(jnp.float32) + jnp.dot(dec_attended, dec_out, preferred_element_type=jnp.float32)).astype(jnp.bfloat16)
    dec_final = feed_forward(dec_mid, dec_norm2, dec_fc1, dec_fc2, rms_norm)
    next_triple = jnp.dot(rms_norm(dec_final, next_norm), next_qkv.reshape(D, 3 * D), preferred_element_type=jnp.float32).astype(jnp.bfloat16)
    return next_triple.reshape(SEQ, 3, D)
```

```python
import jax
import jax.numpy as jnp
from jax import lax
from jax.experimental import pallas as pl
from jax.experimental.pallas import tpu as pltpu
from jax.sharding import PartitionSpec as P

HEAD_DIM = 88


norm_eps = 1e-06


def layer_norm(values, gain_row):
    values = values.astype(jnp.float32)
    centre = values - jnp.mean(values, axis=-1, keepdims=True)
    spread = jnp.mean(centre * centre, axis=-1, keepdims=True)
    return (centre * lax.rsqrt(spread + norm_eps) * gain_row).astype(jnp.bfloat16)


def rms_norm(values, gain_row):
    values = values.astype(jnp.float32)
    square = jnp.mean(values * values, axis=-1, keepdims=True)
    return (values * lax.rsqrt(square + norm_eps) * gain_row).astype(jnp.bfloat16)


def image_bounds(grid_rows):
    merged_count = grid_rows[:, 0] * grid_rows[:, 1]
    merged_end = jnp.cumsum(merged_count)
    return (merged_count, merged_end)


def patch_images(grid_rows, patch_slots):
    merged_count, merged_end = image_bounds(grid_rows)
    slot_index = jnp.arange(patch_slots, dtype=jnp.int32)
    return jnp.sum((slot_index[:, None] >= 4 * merged_end[None, :]).astype(jnp.int32), axis=1)


def merge_sources(grid_rows, merge_slots):
    image_count = grid_rows.shape[0]
    merged_count, merged_end = image_bounds(grid_rows)
    merged_start = merged_end - merged_count
    slot_index = jnp.arange(merge_slots, dtype=jnp.int32)
    image_of = jnp.sum((slot_index[:, None] >= merged_end[None, :]).astype(jnp.int32), axis=1)
    is_live = image_of < image_count
    picked = (
        jnp.minimum(image_of, image_count - 1)[:, None]
        == jnp.arange(image_count, dtype=jnp.int32)[None, :]
    ).astype(jnp.int32)
    col_count = jnp.sum(picked * grid_rows[None, :, 1], axis=1)
    first_slot = jnp.sum(picked * merged_start[None, :], axis=1)
    local_slot = slot_index - first_slot
    grid_row = local_slot // col_count
    grid_col = local_slot % col_count
    base_row = 4 * first_slot + 4 * grid_row * col_count + 2 * grid_col
    offsets = jnp.stack(
        [jnp.zeros_like(col_count), jnp.ones_like(col_count), 2 * col_count, 2 * col_count + 1],
        axis=1,
    )
    return jnp.where(is_live[:, None], base_row[:, None] + offsets, 0)


def request_of(index_rows, bounds):
    return jnp.sum((index_rows[:, None] >= bounds[None, :]).astype(jnp.int32), axis=1)


def local_heads(queries, key_rows, value_rows, allowed):
    scores = jnp.einsum(
        "qhe,khe->hqk", queries, key_rows, preferred_element_type=jnp.float32
    ) * HEAD_DIM ** (-0.5)
    exp_scores = jnp.where(allowed[None], jnp.exp(scores), 0.0)
    denominator = jnp.sum(exp_scores, axis=2)
    weighted = jnp.einsum(
        "hqk,khe->qhe",
        exp_scores.astype(jnp.bfloat16),
        value_rows,
        preferred_element_type=jnp.float32,
    )
    result = (weighted / denominator.T[:, :, None]).astype(jnp.bfloat16)
    return result.reshape(queries.shape[0], -1)


Z_COUNT = 4
MESH = pl.DeviceIdType.MESH


def grid_of(count):
    tall = Z_COUNT if count % Z_COUNT == 0 else 1
    return tall, count // tall


def column_parts(width):
    first = (width // 128 + 1) // 2 * 128
    return pl.ds(0, first), pl.ds(first, width - first)


def greet(places):
    barrier = pltpu.get_barrier_semaphore()
    for present, peer in places:
        @pl.when(present)
        def _():
            pl.semaphore_signal(barrier, inc=1, device_id={"gy": peer}, device_id_type=MESH)
    pl.semaphore_wait(barrier, sum(jnp.where(present, 1, 0) for present, peer in places))


def neighbours(z, x, z_count, x_count):
    return (
        (z > 0, jnp.maximum(z - 1, 0) * x_count + x),
        (z < z_count - 1, jnp.minimum(z + 1, z_count - 1) * x_count + x),
        (x > 0, z * x_count + jnp.maximum(x - 1, 0)),
        (x < x_count - 1, z * x_count + jnp.minimum(x + 1, x_count - 1)),
    )


def line_gather(count, pos, device_of, view, sends, recvs):
    last = count - 1
    for step in range(count - 1):
        moves = []
        for way in (0, 1):
            toward = 1 if way == 0 else -1
            own = pos - toward * step
            peer = pos + toward
            come = pos - toward * (step + 1)
            sending = (own >= 0) & (own <= last) & (peer >= 0) & (peer <= last)
            coming = (come >= 0) & (come <= last)
            peer = jnp.clip(peer, 0, last)

            def copy_of(index, peer=peer, way=way, step=step):
                part = view(jnp.clip(index, 0, last))
                return pltpu.make_async_remote_copy(
                    src_ref=part,
                    dst_ref=part,
                    send_sem=sends.at[way, step],
                    recv_sem=recvs.at[way, step],
                    device_id={"gy": device_of(peer)},
                    device_id_type=MESH,
                )

            @pl.when(sending)
            def _():
                copy_of(own).start()

            moves.append((sending, own, coming, come, copy_of))
        yield
        for sending, own, coming, come, copy_of in moves:
            @pl.when(coming)
            def _():
                copy_of(come).wait_recv()
        yield
        for sending, own, coming, come, copy_of in moves:
            @pl.when(sending)
            def _():
                copy_of(own).wait_send()


def chain(*lines):
    for line in lines:
        yield from line


def run_together(*lines):
    lines = list(lines)
    while lines:
        for line in list(lines):
            try:
                next(line)
            except StopIteration:
                lines.remove(line)


def gather_kernel(z_count, x_count, block, out, *sems):
    me = lax.axis_index("gy")
    z, x = me // x_count, me % x_count
    greet(neighbours(z, x, z_count, x_count))
    out[z, x] = block[...]
    left, right = column_parts(block.shape[1])

    def along_z(k):
        return k * x_count + x

    def along_x(k):
        return z * x_count + k

    run_together(
        chain(
            line_gather(z_count, z, along_z, lambda k: out.at[k, x, :, left], sems[0], sems[1]),
            line_gather(
                x_count, x, along_x, lambda k: out.at[:, k, :, left], sems[2], sems[3]
            ),
        ),
        chain(
            line_gather(x_count, x, along_x, lambda k: out.at[z, k, :, right], sems[4], sems[5]),
            line_gather(
                z_count, z, along_z, lambda k: out.at[k, :, :, right], sems[6], sems[7]
            ),
        ),
    )


def line_reduce(count, pos, device_of, own, store, outgoing, incoming, sends, recvs):
    last = count - 1
    for step in range(count - 1):
        moves = []
        for way in (0, 1):
            toward = 1 if way == 0 else -1
            dest = last - step if way == 0 else step
            peer = jnp.clip(pos + toward, 0, last)
            sending = pos < dest if way == 0 else pos > dest
            fed = (pos > 0) if way == 0 else (pos < last)
            coming = fed & ((pos <= dest) if way == 0 else (pos >= dest))
            copy = pltpu.make_async_remote_copy(
                src_ref=outgoing.at[way, step],
                dst_ref=incoming.at[way, step],
                send_sem=sends.at[way, step],
                recv_sem=recvs.at[way, step],
                device_id={"gy": device_of(peer)},
                device_id_type=MESH,
            )
            moves.append((sending, fed, coming, copy, dest, way))
        for sending, fed, coming, copy, dest, way in moves:
            @pl.when(coming)
            def _():
                copy.wait_recv()

            @pl.when(sending & fed)
            def _():
                outgoing[way, step] = (own(dest) + incoming[way, step].astype(jnp.float32)).astype(
                    jnp.bfloat16
                )

            @pl.when(sending & jnp.logical_not(fed))
            def _():
                outgoing[way, step] = own(dest).astype(jnp.bfloat16)

            @pl.when(sending)
            def _():
                copy.start()
        yield
        for sending, fed, coming, copy, dest, way in moves:
            @pl.when(sending)
            def _():
                copy.wait_send()
    store(own(pos))
    for way in (0, 1):
        step_of = last - pos if way == 0 else pos

        @pl.when(pos > 0 if way == 0 else pos < last)
        def _():
            kept = jnp.clip(step_of, 0, max(last - 1, 0))
            store(None, incoming[way, kept].astype(jnp.float32))
    yield


def reduce_kernel(z_count, x_count, terms, out, sum_l, sum_r, total_l, total_r, *rest):
    bufs, sems = rest[:8], rest[8:]
    me = lax.axis_index("gy")
    z, x = me // x_count, me % x_count
    greet(neighbours(z, x, z_count, x_count))
    left, right = column_parts(terms.shape[3])

    def along_z(k):
        return k * x_count + x

    def along_x(k):
        return z * x_count + k

    def keep(ref):
        def store(first, more=None):
            if more is None:
                ref[...] = first
            else:
                ref[...] += more

        return store

    run_together(
        chain(
            line_reduce(
                x_count, x, along_x, lambda k: terms[:, k, :, left].astype(jnp.float32),
                keep(sum_l), bufs[0], bufs[1], sems[0], sems[1],
            ),
            line_reduce(
                z_count, z, along_z, lambda k: sum_l[k], keep(total_l),
                bufs[2], bufs[3], sems[2], sems[3],
            ),
        ),
        chain(
            line_reduce(
                z_count, z, along_z, lambda k: terms[k, :, :, right].astype(jnp.float32),
                keep(sum_r), bufs[4], bufs[5], sems[4], sems[5],
            ),
            line_reduce(
                x_count, x, along_x, lambda k: sum_r[k], keep(total_r),
                bufs[6], bufs[7], sems[6], sems[7],
            ),
        ),
    )
    out[:, left] = total_l[...]
    out[:, right] = total_r[...]


def swap_kernel(count, blocks, out, sends, recvs):
    me = lax.axis_index("gy")
    barrier = pltpu.get_barrier_semaphore()
    for shift in range(1, count):
        peer = lax.rem(me + shift, count)
        pl.semaphore_signal(barrier, inc=1, device_id={"gy": peer}, device_id_type=MESH)
    pl.semaphore_wait(barrier, count - 1)
    copies = []
    for shift in range(1, count):
        peer = lax.rem(me + shift, count)
        copy = pltpu.make_async_remote_copy(
            src_ref=blocks.at[peer],
            dst_ref=out.at[me],
            send_sem=sends.at[shift - 1],
            recv_sem=recvs.at[shift - 1],
            device_id={"gy": peer},
            device_id_type=MESH,
        )
        copy.start()
        copies.append(copy)
    out[me] = blocks[me]
    for copy in copies:
        copy.wait_recv()
    for copy in copies:
        copy.wait_send()


def call(body, out_shape, scratch, identity, name, size):
    whole = pl.BlockSpec(memory_space=pltpu.VMEM)
    return pl.pallas_call(
        body,
        out_shape=out_shape,
        in_specs=[whole],
        out_specs=whole,
        scratch_shapes=scratch,
        name=name,
        cost_estimate=pl.CostEstimate(flops=0, bytes_accessed=size, transcendentals=0),
        compiler_params=pltpu.CompilerParams(
            collective_id=identity, has_side_effects=True, vmem_limit_bytes=48 * 1024 * 1024
        ),
    )


def pair(count):
    sems = pltpu.SemaphoreType.DMA((2, max(count - 1, 1)))
    return [sems, sems]


def gather_rows(block, identity):
    z_count, x_count = grid_of(lax.axis_size("gy"))
    rows, width = block.shape
    scratch = pair(z_count) + pair(x_count) + pair(x_count) + pair(z_count)
    out = call(
        lambda *refs: gather_kernel(z_count, x_count, *refs),
        jax.ShapeDtypeStruct((z_count, x_count, rows, width), jnp.bfloat16),
        scratch, identity, "gather_rows", 60000000,
    )(block)
    return out.reshape(z_count * x_count * rows, width)


def sum_rows(terms, identity):
    z_count, x_count = grid_of(lax.axis_size("gy"))
    width = terms.shape[1]
    rows = terms.shape[0] // (z_count * x_count)
    left, right = column_parts(width)
    l_size, r_size = left.size, right.size

    def slots(count, *shape):
        slot = pltpu.VMEM((2, max(count - 1, 1)) + shape, jnp.bfloat16)
        return [slot, slot]

    scratch = (
        [
            pltpu.VMEM((z_count, rows, l_size), jnp.float32),
            pltpu.VMEM((x_count, rows, r_size), jnp.float32),
            pltpu.VMEM((rows, l_size), jnp.float32),
            pltpu.VMEM((rows, r_size), jnp.float32),
        ]
        + slots(x_count, z_count, rows, l_size)
        + slots(z_count, rows, l_size)
        + slots(z_count, x_count, rows, r_size)
        + slots(x_count, rows, r_size)
        + pair(x_count) + pair(z_count) + pair(z_count) + pair(x_count)
    )
    return call(
        lambda *refs: reduce_kernel(z_count, x_count, *refs),
        jax.ShapeDtypeStruct((rows, width), jnp.float32),
        scratch, identity, "sum_rows", 60000000,
    )(terms.reshape(z_count, x_count, rows, width))


def swap_to_rows(values, identity):
    count = lax.axis_size("gy")
    rows, width = values.shape[0] // count, values.shape[1]
    sems = pltpu.SemaphoreType.DMA((count - 1,))
    out = call(
        lambda *refs: swap_kernel(count, *refs),
        jax.ShapeDtypeStruct((count, rows, width), jnp.bfloat16),
        [sems, sems], identity, "swap_to_rows", 20000000,
    )(values.reshape(count, rows, width))
    return out.transpose(1, 0, 2)


def full_weight(weight):
    rows, width = weight.shape
    everywhere = lax.all_gather(weight, ("gx", "gy"), axis=0, tiled=False)
    gx_count, gy_count = lax.axis_size("gx"), lax.axis_size("gy")
    return (
        everywhere.reshape(gx_count, gy_count, rows, width)
        .transpose(0, 2, 1, 3)
        .reshape(gx_count * rows, gy_count * width)
    )


def weight_columns(weight):
    return lax.all_gather(weight.reshape(weight.shape[0], -1), "gx", axis=0, tiled=True)


def dense(rows, weight):
    return jnp.dot(rows, weight, preferred_element_type=jnp.float32)


def feed_forward(normed_full, fc_in, fc_back, identity):
    hidden = jax.nn.gelu(dense(normed_full, fc_in), approximate=False).astype(jnp.bfloat16)
    partial_sum = lax.dot_general(
        hidden, fc_back, (((1,), (1,)), ((), ())), preferred_element_type=jnp.float32
    )
    return sum_rows(partial_sum.astype(jnp.bfloat16), identity)


def per_device(
    patches,
    grids,
    text_ids,
    positions,
    lengths,
    text_table,
    vit_norm1,
    vit_qkv,
    vit_out,
    vit_norm2,
    vit_fc1,
    vit_fc2,
    merge_norm,
    merge_proj,
    dec_norm1,
    dec_qkv,
    dec_out,
    dec_norm2,
    dec_fc1,
    dec_fc2,
    next_norm,
    next_qkv,
):
    gx_count = lax.axis_size("gx")
    gx_index = lax.axis_index("gx")
    gy_count = lax.axis_size("gy")
    gy_index = lax.axis_index("gy")
    per_group = grids.shape[0] // gx_count
    own_grids = lax.dynamic_slice_in_dim(grids, gx_index * per_group, per_group, 0)
    local_width = vit_qkv.shape[2]
    head_count = local_width // HEAD_DIM
    vit_qkv, vit_fc1, vit_fc2, merge_proj, dec_qkv, dec_fc1, dec_fc2, next_qkv = [
        weight_columns(weight)
        for weight in (vit_qkv, vit_fc1, vit_fc2, merge_proj, dec_qkv, dec_fc1, dec_fc2, next_qkv)
    ]
    vit_out, dec_out = full_weight(vit_out), full_weight(dec_out)

    patches_full = gather_rows(patches, 0)
    patch_slots, full_width = patches_full.shape
    merge_slots = positions.shape[0] // gx_count
    sources = merge_sources(own_grids, merge_slots).reshape(merge_slots * 4)
    slot_index = jnp.arange(patch_slots, dtype=jnp.int32)
    chosen = (sources[:, None] == slot_index[None, :]).astype(jnp.bfloat16)
    ordered = dense(chosen, patches_full).astype(jnp.bfloat16)
    triple = dense(layer_norm(ordered, vit_norm1), vit_qkv).astype(jnp.bfloat16)
    triple = triple.reshape(patch_slots, 3, head_count, HEAD_DIM)
    image_ids = jnp.sum(
        (sources[:, None] >= 4 * image_bounds(own_grids)[1][None, :]).astype(jnp.int32), axis=1
    )
    is_key = slot_index < 4 * jnp.sum(own_grids[:, 0] * own_grids[:, 1])
    attended = local_heads(
        triple[:, 0],
        triple[:, 1],
        triple[:, 2],
        (image_ids[:, None] == image_ids[None, :]) & is_key[None, :],
    )
    own_rows = patch_slots // gy_count
    patches_own = lax.dynamic_slice_in_dim(ordered, gy_index * own_rows, own_rows, 0)
    attended_own = swap_to_rows(attended, 1).reshape(own_rows, full_width)
    vit_mid = (patches_own.astype(jnp.float32) + dense(attended_own, vit_out)).astype(jnp.bfloat16)
    vit_normed = gather_rows(layer_norm(vit_mid, vit_norm2), 2)
    summed = feed_forward(vit_normed, vit_fc1, vit_fc2, 3)
    vit_final = (vit_mid.astype(jnp.float32) + summed).astype(jnp.bfloat16)
    merged = vit_final.astype(jnp.float32).reshape(own_rows // 4, 4, full_width)
    centre = merged - jnp.mean(merged, axis=(1, 2), keepdims=True)
    spread = jnp.mean(centre * centre, axis=(1, 2), keepdims=True)
    merged_normed = (centre * lax.rsqrt(spread + norm_eps) * merge_norm).astype(jnp.bfloat16)
    merged_full = gather_rows(merged_normed.reshape(own_rows, full_width), 4)
    products = dense(merged_full, merge_proj).reshape(merge_slots, 4, 4 * local_width)
    projected = products[:, 0, :local_width]
    for k in range(1, 4):
        projected = projected + products[:, k, k * local_width : (k + 1) * local_width]
    projected = projected.astype(jnp.bfloat16)

    seq_slots = text_ids.shape[0]
    seq_rows = seq_slots // gy_count
    seq_index = gx_index * seq_slots + jnp.arange(seq_slots, dtype=jnp.int32)
    matches = positions[None, :] == seq_index[:, None]
    all_projected = lax.all_gather(projected, "gx", axis=0, tiled=True)
    placed = dense(matches.astype(jnp.bfloat16), all_projected).astype(jnp.bfloat16)
    placed_own = swap_to_rows(placed, 5).reshape(seq_rows, full_width)
    vocab_rows = text_table.shape[0]
    shifted_ids = text_ids - gy_index * vocab_rows
    inside = (shifted_ids >= 0) & (shifted_ids < vocab_rows)
    looked_up = jnp.take(text_table, jnp.clip(shifted_ids, 0, vocab_rows - 1), axis=0)
    table_terms = jnp.where(inside[:, None], looked_up, jnp.bfloat16(0))
    text_own = sum_rows(table_terms, 6).astype(jnp.bfloat16)
    is_image = lax.dynamic_slice_in_dim(
        jnp.any(matches, axis=1), gy_index * seq_rows, seq_rows, 0
    )
    embedded = jnp.where(is_image[:, None], placed_own, text_own)

    dec_normed = gather_rows(rms_norm(embedded, dec_norm1), 7)
    dec_triple = dense(dec_normed, dec_qkv).astype(jnp.bfloat16)
    queries = dec_triple[:, :local_width].reshape(seq_slots, head_count, HEAD_DIM)
    bounds = jnp.cumsum(lengths)
    own_request = request_of(seq_index, bounds)
    pairs = lax.all_gather(dec_triple[:, local_width:], "gx", axis=0, tiled=True)
    key_count = pairs.shape[0]
    pairs = pairs.reshape(key_count, 2, head_count, HEAD_DIM)
    key_index = jnp.arange(key_count, dtype=jnp.int32)
    allowed = (request_of(key_index, bounds)[None, :] == own_request[:, None]) & (
        key_index[None, :] <= seq_index[:, None]
    )
    dec_attended = local_heads(queries, pairs[:, 0], pairs[:, 1], allowed)
    dec_own = swap_to_rows(dec_attended, 8).reshape(seq_rows, full_width)
    dec_mid = (embedded.astype(jnp.float32) + dense(dec_own, dec_out)).astype(jnp.bfloat16)
    mid_normed = gather_rows(rms_norm(dec_mid, dec_norm2), 9)
    summed = feed_forward(mid_normed, dec_fc1, dec_fc2, 10)
    dec_final = (dec_mid.astype(jnp.float32) + summed).astype(jnp.bfloat16)
    next_normed = gather_rows(rms_norm(dec_final, next_norm), 11)
    next_local = dense(next_normed, next_qkv).astype(jnp.bfloat16)
    next_own = swap_to_rows(next_local, 12).reshape(seq_rows, gy_count, 3, local_width)
    return next_own.transpose(0, 2, 1, 3).reshape(seq_rows, 3, full_width)


def solution(mesh):
    placed = (
        P(("gx", "gy"), None),
        P(),
        P("gx"),
        P(),
        P(),
        P("gy", None),
        P(),
        P("gx", None, "gy"),
        P("gx", "gy"),
        P(),
        P("gx", "gy"),
        P("gx", "gy"),
        P(),
        P("gx", None, "gy"),
        P(),
        P("gx", None, "gy"),
        P("gx", "gy"),
        P(),
        P("gx", "gy"),
        P("gx", "gy"),
        P(),
        P("gx", None, "gy"),
    )
    return jax.shard_map(
        per_device,
        mesh=mesh,
        in_specs=placed,
        out_specs=P(("gx", "gy"), None, None),
        check_vma=False,
    )
```

```python
import jax
import jax.numpy as jnp
from jax import lax
from jax.experimental import pallas as pl
from jax.experimental.pallas import tpu as pltpu
from jax.sharding import PartitionSpec as P

HEAD_DIM = 88


norm_eps = 1e-06


def layer_norm(values, gain_row):
    values = values.astype(jnp.float32)
    centre = values - jnp.mean(values, axis=-1, keepdims=True)
    spread = jnp.mean(centre * centre, axis=-1, keepdims=True)
    return (centre * lax.rsqrt(spread + norm_eps) * gain_row).astype(jnp.bfloat16)


def rms_norm(values, gain_row):
    values = values.astype(jnp.float32)
    square = jnp.mean(values * values, axis=-1, keepdims=True)
    return (values * lax.rsqrt(square + norm_eps) * gain_row).astype(jnp.bfloat16)


def image_bounds(grid_rows):
    merged_count = grid_rows[:, 0] * grid_rows[:, 1]
    merged_end = jnp.cumsum(merged_count)
    return (merged_count, merged_end)


def patch_images(grid_rows, patch_slots):
    merged_count, merged_end = image_bounds(grid_rows)
    slot_index = jnp.arange(patch_slots, dtype=jnp.int32)
    return jnp.sum((slot_index[:, None] >= 4 * merged_end[None, :]).astype(jnp.int32), axis=1)


def merge_sources(grid_rows, merge_slots):
    image_count = grid_rows.shape[0]
    merged_count, merged_end = image_bounds(grid_rows)
    merged_start = merged_end - merged_count
    slot_index = jnp.arange(merge_slots, dtype=jnp.int32)
    image_of = jnp.sum((slot_index[:, None] >= merged_end[None, :]).astype(jnp.int32), axis=1)
    is_live = image_of < image_count
    picked = (
        jnp.minimum(image_of, image_count - 1)[:, None]
        == jnp.arange(image_count, dtype=jnp.int32)[None, :]
    ).astype(jnp.int32)
    col_count = jnp.sum(picked * grid_rows[None, :, 1], axis=1)
    first_slot = jnp.sum(picked * merged_start[None, :], axis=1)
    local_slot = slot_index - first_slot
    grid_row = local_slot // col_count
    grid_col = local_slot % col_count
    base_row = 4 * first_slot + 4 * grid_row * col_count + 2 * grid_col
    offsets = jnp.stack(
        [jnp.zeros_like(col_count), jnp.ones_like(col_count), 2 * col_count, 2 * col_count + 1],
        axis=1,
    )
    return jnp.where(is_live[:, None], base_row[:, None] + offsets, 0)


def request_of(index_rows, bounds):
    return jnp.sum((index_rows[:, None] >= bounds[None, :]).astype(jnp.int32), axis=1)


def local_heads(queries, key_rows, value_rows, allowed):
    scores = jnp.einsum(
        "qhe,khe->hqk", queries, key_rows, preferred_element_type=jnp.float32
    ) * HEAD_DIM ** (-0.5)
    exp_scores = jnp.where(allowed[None], jnp.exp(scores), 0.0)
    denominator = jnp.sum(exp_scores, axis=2)
    weighted = jnp.einsum(
        "hqk,khe->qhe",
        exp_scores.astype(jnp.bfloat16),
        value_rows,
        preferred_element_type=jnp.float32,
    )
    result = (weighted / denominator.T[:, :, None]).astype(jnp.bfloat16)
    return result.reshape(queries.shape[0], -1)


Z_COUNT = 4
MESH = pl.DeviceIdType.MESH


def grid_of(count):
    tall = Z_COUNT if count % Z_COUNT == 0 else 1
    return tall, count // tall


def column_parts(width, z_count, x_count):
    tiles = width // 128
    first = (tiles * 5 // 6 if 2 * x_count <= z_count else (tiles + 1) // 2) * 128
    return pl.ds(0, first), pl.ds(first, width - first)


def greet(places):
    barrier = pltpu.get_barrier_semaphore()
    for present, peer in places:
        @pl.when(present)
        def _():
            pl.semaphore_signal(barrier, inc=1, device_id={"gy": peer}, device_id_type=MESH)
    pl.semaphore_wait(barrier, sum(jnp.where(present, 1, 0) for present, peer in places))


def neighbours(z, x, z_count, x_count):
    return (
        (z > 0, jnp.maximum(z - 1, 0) * x_count + x),
        (z < z_count - 1, jnp.minimum(z + 1, z_count - 1) * x_count + x),
        (x > 0, z * x_count + jnp.maximum(x - 1, 0)),
        (x < x_count - 1, z * x_count + jnp.minimum(x + 1, x_count - 1)),
    )


def line_gather(count, pos, device_of, view, sends, recvs, enabled=None, arrived=None):
    last = count - 1
    sent = []
    for step in range(count - 1):
        moves = []
        for way in (0, 1):
            toward = 1 if way == 0 else -1
            own = pos - toward * step
            peer = pos + toward
            come = pos - toward * (step + 1)
            sending = (own >= 0) & (own <= last) & (peer >= 0) & (peer <= last)
            coming = (come >= 0) & (come <= last)
            if enabled is not None:
                sending, coming = sending & enabled, coming & enabled
            peer = jnp.clip(peer, 0, last)

            def copy_of(index, peer=peer, way=way, step=step):
                part = view(jnp.clip(index, 0, last))
                return pltpu.make_async_remote_copy(
                    src_ref=part,
                    dst_ref=part,
                    send_sem=sends(way, step),
                    recv_sem=recvs(way, step),
                    device_id={"gy": device_of(peer)},
                    device_id_type=MESH,
                )

            @pl.when(sending)
            def _():
                copy_of(own).start()

            moves.append((coming, come, copy_of, way))
            sent.append((sending, own, copy_of))
        yield
        for coming, come, copy_of, way in moves:
            @pl.when(coming)
            def _():
                copy_of(come).wait_recv()

            if arrived is not None:
                arrived(step, way, jnp.clip(come, 0, last), coming)
        yield
    for sending, own, copy_of in sent:
        @pl.when(sending)
        def _():
            copy_of(own).wait_send()


def chain(*lines):
    for line in lines:
        yield from line


def run_together(*lines):
    lines = list(lines)
    while lines:
        for line in list(lines):
            try:
                next(line)
            except StopIteration:
                lines.remove(line)


def gather_kernel(z_count, x_count, block, out, *sems):
    me = lax.axis_index("gy")
    z, x = me // x_count, me % x_count
    greet(neighbours(z, x, z_count, x_count))
    left, right = column_parts(block.shape[1], z_count, x_count)

    def along_z(k):
        return k * x_count + x

    def along_x(k):
        return z * x_count + k

    def pick(ref, *lead):
        return lambda way, step: ref.at[(*lead, way, step)]

    out[z, x] = block[...]

    def z_first():
        pending = []

        def onward(k, enabled, slot):
            line = line_gather(
                x_count, x, along_x, lambda q: out.at[k, q, :, left],
                pick(sems[2], slot), pick(sems[3], slot), enabled,
            )
            next(line, None)
            pending.append(line)

        onward(z, None, 0)
        yield from line_gather(
            z_count, z, along_z, lambda k: out.at[k, x, :, left], pick(sems[0]), pick(sems[1]),
            arrived=lambda step, way, k, coming: onward(k, coming, 1 + 2 * step + way),
        )
        for line in pending:
            yield from line

    run_together(
        z_first(),
        chain(
            line_gather(
                x_count, x, along_x, lambda k: out.at[z, k, :, right], pick(sems[4]), pick(sems[5])
            ),
            line_gather(
                z_count, z, along_z, lambda k: out.at[k, :, :, right], pick(sems[6]), pick(sems[7])
            ),
        ),
    )


def line_reduce(count, pos, device_of, own, store, outgoing, incoming, sends, recvs):
    last = count - 1

    def copy_of(way, slot):
        return pltpu.make_async_remote_copy(
            src_ref=outgoing.at[way, slot],
            dst_ref=incoming.at[way, slot],
            send_sem=sends.at[way, slot],
            recv_sem=recvs.at[way, slot],
            device_id={"gy": device_of(jnp.clip(pos + (1 if way == 0 else -1), 0, last))},
            device_id_type=MESH,
        )

    behind = (pos, last - pos)
    for time in range(count - 1):
        for way in (0, 1):
            slot = jnp.clip(time - behind[way], 0, last - 1)
            dest = last - slot if way == 0 else slot

            @pl.when((behind[way] > 0) & (behind[way] <= time))
            def _():
                copy_of(way, slot).wait_recv()
                outgoing[way, slot] = (
                    own(dest) + incoming[way, slot].astype(jnp.float32)
                ).astype(jnp.bfloat16)
                copy_of(way, slot).start()

            @pl.when(behind[way] == 0)
            def _():
                outgoing[way, slot] = own(dest).astype(jnp.bfloat16)
                copy_of(way, slot).start()

        yield
    store(own(pos))
    yield
    for way in (0, 1):
        @pl.when(behind[way] > 0)
        def _():
            slot = jnp.clip(last - behind[way], 0, max(last - 1, 0))
            copy_of(way, slot).wait_recv()
            store(None, incoming[way, slot].astype(jnp.float32))
    for time in range(count - 1):
        for way in (0, 1):
            @pl.when(behind[way] <= time)
            def _():
                copy_of(way, jnp.clip(time - behind[way], 0, last - 1)).wait_send()


def reduce_kernel(z_count, x_count, terms, out, sum_l, sum_r, total_l, total_r, *rest):
    bufs, sems = rest[:8], rest[8:]
    me = lax.axis_index("gy")
    z, x = me // x_count, me % x_count
    greet(neighbours(z, x, z_count, x_count))
    left, right = column_parts(terms.shape[3], z_count, x_count)

    def along_z(k):
        return k * x_count + x

    def along_x(k):
        return z * x_count + k

    def keep(ref):
        def store(first, more=None):
            if more is None:
                ref[...] = first
            else:
                ref[...] += more

        return store

    run_together(
        chain(
            line_reduce(
                x_count, x, along_x, lambda k: terms[:, k, :, left].astype(jnp.float32),
                keep(sum_l), bufs[0], bufs[1], sems[0], sems[1],
            ),
            line_reduce(
                z_count, z, along_z, lambda k: sum_l[k], keep(total_l),
                bufs[2], bufs[3], sems[2], sems[3],
            ),
        ),
        chain(
            line_reduce(
                z_count, z, along_z, lambda k: terms[k, :, :, right].astype(jnp.float32),
                keep(sum_r), bufs[4], bufs[5], sems[4], sems[5],
            ),
            line_reduce(
                x_count, x, along_x, lambda k: sum_r[k], keep(total_r),
                bufs[6], bufs[7], sems[6], sems[7],
            ),
        ),
    )
    out[:, left] = total_l[...]
    out[:, right] = total_r[...]


def swap_kernel(count, blocks, out, sends, recvs):
    me = lax.axis_index("gy")
    barrier = pltpu.get_barrier_semaphore()
    for shift in range(1, count):
        peer = lax.rem(me + shift, count)
        pl.semaphore_signal(barrier, inc=1, device_id={"gy": peer}, device_id_type=MESH)
    pl.semaphore_wait(barrier, count - 1)
    copies = []
    for shift in range(1, count):
        peer = lax.rem(me + shift, count)
        copy = pltpu.make_async_remote_copy(
            src_ref=blocks.at[peer],
            dst_ref=out.at[me],
            send_sem=sends.at[shift - 1],
            recv_sem=recvs.at[shift - 1],
            device_id={"gy": peer},
            device_id_type=MESH,
        )
        copy.start()
        copies.append(copy)
    out[me] = blocks[me]
    for copy in copies:
        copy.wait_recv()
    for copy in copies:
        copy.wait_send()


def call(body, out_shape, scratch, identity, name, size):
    whole = pl.BlockSpec(memory_space=pltpu.VMEM)
    return pl.pallas_call(
        body,
        out_shape=out_shape,
        in_specs=[whole],
        out_specs=whole,
        scratch_shapes=scratch,
        name=name,
        cost_estimate=pl.CostEstimate(flops=0, bytes_accessed=size, transcendentals=0),
        compiler_params=pltpu.CompilerParams(
            collective_id=identity, has_side_effects=True, vmem_limit_bytes=48 * 1024 * 1024
        ),
    )


def pair(count, *lead):
    sems = pltpu.SemaphoreType.DMA((*lead, 2, max(count - 1, 1)))
    return [sems, sems]


def gather_rows(block, identity):
    z_count, x_count = grid_of(lax.axis_size("gy"))
    rows, width = block.shape
    scratch = pair(z_count) + pair(x_count, 2 * z_count - 1) + pair(x_count) + pair(z_count)
    out = call(
        lambda *refs: gather_kernel(z_count, x_count, *refs),
        jax.ShapeDtypeStruct((z_count, x_count, rows, width), jnp.bfloat16),
        scratch, identity, "gather_rows", 60000000,
    )(block)
    return out.reshape(z_count * x_count * rows, width)


def sum_rows(terms, identity):
    z_count, x_count = grid_of(lax.axis_size("gy"))
    width = terms.shape[1]
    rows = terms.shape[0] // (z_count * x_count)
    left, right = column_parts(width, z_count, x_count)
    l_size, r_size = left.size, right.size

    def slots(count, *shape):
        slot = pltpu.VMEM((2, max(count - 1, 1)) + shape, jnp.bfloat16)
        return [slot, slot]

    scratch = (
        [
            pltpu.VMEM((z_count, rows, l_size), jnp.float32),
            pltpu.VMEM((x_count, rows, r_size), jnp.float32),
            pltpu.VMEM((rows, l_size), jnp.float32),
            pltpu.VMEM((rows, r_size), jnp.float32),
        ]
        + slots(x_count, z_count, rows, l_size)
        + slots(z_count, rows, l_size)
        + slots(z_count, x_count, rows, r_size)
        + slots(x_count, rows, r_size)
        + pair(x_count) + pair(z_count) + pair(z_count) + pair(x_count)
    )
    return call(
        lambda *refs: reduce_kernel(z_count, x_count, *refs),
        jax.ShapeDtypeStruct((rows, width), jnp.float32),
        scratch, identity, "sum_rows", 60000000,
    )(terms.reshape(z_count, x_count, rows, width))


def swap_to_rows(values, identity):
    count = lax.axis_size("gy")
    rows, width = values.shape[0] // count, values.shape[1]
    sems = pltpu.SemaphoreType.DMA((count - 1,))
    out = call(
        lambda *refs: swap_kernel(count, *refs),
        jax.ShapeDtypeStruct((count, rows, width), jnp.bfloat16),
        [sems, sems], identity, "swap_to_rows", 20000000,
    )(values.reshape(count, rows, width))
    return out.transpose(1, 0, 2)


def full_weight(weight):
    return lax.all_gather(weight, ("gx", "gy"), axis=0, tiled=False)


def full_product(rows, blocks):
    gx_count, gy_count = lax.axis_size("gx"), lax.axis_size("gy")
    depth, width = blocks.shape[1:]
    total = jnp.zeros((gy_count, rows.shape[0], width), jnp.float32)
    for i in range(gx_count):
        part = rows[:, i * depth : (i + 1) * depth]
        total = total + jnp.einsum(
            "jtk,jkn->jtn",
            jnp.broadcast_to(part[None], (gy_count,) + part.shape),
            blocks[i * gy_count : (i + 1) * gy_count],
            preferred_element_type=jnp.float32,
        )
    return total.transpose(1, 0, 2).reshape(rows.shape[0], gy_count * width)


def weight_columns(weight):
    return lax.all_gather(weight.reshape(weight.shape[0], -1), "gx", axis=0, tiled=True)


def dense(rows, weight):
    return jnp.dot(rows, weight, preferred_element_type=jnp.float32)


def feed_forward(normed_full, fc_in, fc_back, identity):
    hidden = jax.nn.gelu(dense(normed_full, fc_in), approximate=False).astype(jnp.bfloat16)
    partial_sum = lax.dot_general(
        hidden, fc_back, (((1,), (1,)), ((), ())), preferred_element_type=jnp.float32
    )
    return sum_rows(partial_sum.astype(jnp.bfloat16), identity)


def per_device(
    patches,
    grids,
    text_ids,
    positions,
    lengths,
    text_table,
    vit_norm1,
    vit_qkv,
    vit_out,
    vit_norm2,
    vit_fc1,
    vit_fc2,
    merge_norm,
    merge_proj,
    dec_norm1,
    dec_qkv,
    dec_out,
    dec_norm2,
    dec_fc1,
    dec_fc2,
    next_norm,
    next_qkv,
):
    gx_count = lax.axis_size("gx")
    gx_index = lax.axis_index("gx")
    gy_count = lax.axis_size("gy")
    gy_index = lax.axis_index("gy")
    per_group = grids.shape[0] // gx_count
    own_grids = lax.dynamic_slice_in_dim(grids, gx_index * per_group, per_group, 0)
    local_width = vit_qkv.shape[2]
    head_count = local_width // HEAD_DIM
    vit_qkv, vit_fc1, vit_fc2, merge_proj, dec_qkv, dec_fc1, dec_fc2, next_qkv = [
        weight_columns(weight)
        for weight in (vit_qkv, vit_fc1, vit_fc2, merge_proj, dec_qkv, dec_fc1, dec_fc2, next_qkv)
    ]
    vit_out, dec_out = full_weight(vit_out), full_weight(dec_out)

    patches_full = gather_rows(patches, 0)
    patch_slots, full_width = patches_full.shape
    merge_slots = positions.shape[0] // gx_count
    sources = merge_sources(own_grids, merge_slots).reshape(merge_slots * 4)
    slot_index = jnp.arange(patch_slots, dtype=jnp.int32)
    chosen = (sources[:, None] == slot_index[None, :]).astype(jnp.bfloat16)
    ordered = dense(chosen, patches_full).astype(jnp.bfloat16)
    triple = dense(layer_norm(ordered, vit_norm1), vit_qkv).astype(jnp.bfloat16)
    triple = triple.reshape(patch_slots, 3, head_count, HEAD_DIM)
    image_ids = jnp.sum(
        (sources[:, None] >= 4 * image_bounds(own_grids)[1][None, :]).astype(jnp.int32), axis=1
    )
    is_key = slot_index < 4 * jnp.sum(own_grids[:, 0] * own_grids[:, 1])
    attended = local_heads(
        triple[:, 0],
        triple[:, 1],
        triple[:, 2],
        (image_ids[:, None] == image_ids[None, :]) & is_key[None, :],
    )
    own_rows = patch_slots // gy_count
    patches_own = lax.dynamic_slice_in_dim(ordered, gy_index * own_rows, own_rows, 0)
    attended_own = swap_to_rows(attended, 1).reshape(own_rows, full_width)
    vit_mid = (patches_own.astype(jnp.float32) + full_product(attended_own, vit_out)).astype(jnp.bfloat16)
    vit_normed = gather_rows(layer_norm(vit_mid, vit_norm2), 2)
    summed = feed_forward(vit_normed, vit_fc1, vit_fc2, 3)
    vit_final = (vit_mid.astype(jnp.float32) + summed).astype(jnp.bfloat16)
    merged = vit_final.astype(jnp.float32).reshape(own_rows // 4, 4, full_width)
    centre = merged - jnp.mean(merged, axis=(1, 2), keepdims=True)
    spread = jnp.mean(centre * centre, axis=(1, 2), keepdims=True)
    merged_normed = (centre * lax.rsqrt(spread + norm_eps) * merge_norm).astype(jnp.bfloat16)
    merged_full = gather_rows(merged_normed.reshape(own_rows, full_width), 4)
    products = dense(merged_full, merge_proj).reshape(merge_slots, 4, 4 * local_width)
    projected = products[:, 0, :local_width]
    for k in range(1, 4):
        projected = projected + products[:, k, k * local_width : (k + 1) * local_width]
    projected = projected.astype(jnp.bfloat16)

    seq_slots = text_ids.shape[0]
    seq_rows = seq_slots // gy_count
    seq_index = gx_index * seq_slots + jnp.arange(seq_slots, dtype=jnp.int32)
    matches = positions[None, :] == seq_index[:, None]
    all_projected = lax.all_gather(projected, "gx", axis=0, tiled=True)
    placed = dense(matches.astype(jnp.bfloat16), all_projected).astype(jnp.bfloat16)
    placed_own = swap_to_rows(placed, 5).reshape(seq_rows, full_width)
    vocab_rows = text_table.shape[0]
    shifted_ids = text_ids - gy_index * vocab_rows
    inside = (shifted_ids >= 0) & (shifted_ids < vocab_rows)
    looked_up = jnp.take(text_table, jnp.clip(shifted_ids, 0, vocab_rows - 1), axis=0)
    table_terms = jnp.where(inside[:, None], looked_up, jnp.bfloat16(0))
    text_own = sum_rows(table_terms, 6).astype(jnp.bfloat16)
    is_image = lax.dynamic_slice_in_dim(
        jnp.any(matches, axis=1), gy_index * seq_rows, seq_rows, 0
    )
    embedded = jnp.where(is_image[:, None], placed_own, text_own)

    dec_normed = gather_rows(rms_norm(embedded, dec_norm1), 7)
    dec_triple = dense(dec_normed, dec_qkv).astype(jnp.bfloat16)
    bounds = jnp.cumsum(lengths)
    own_request = request_of(seq_index, bounds)
    dec_triple = dec_triple.reshape(seq_slots, 3, local_width)
    key_rows = lax.all_gather(dec_triple[:, 1], "gx", axis=0, tiled=True)
    value_rows = lax.all_gather(dec_triple[:, 2], "gx", axis=0, tiled=True)
    key_count = key_rows.shape[0]
    key_rows = key_rows.reshape(key_count, head_count, HEAD_DIM)
    value_rows = value_rows.reshape(key_count, head_count, HEAD_DIM)
    key_index = jnp.arange(key_count, dtype=jnp.int32)
    allowed = (request_of(key_index, bounds)[None, :] == own_request[:, None]) & (
        key_index[None, :] <= seq_index[:, None]
    )
    queries = dec_triple[:, 0].reshape(seq_slots, head_count, HEAD_DIM)
    dec_attended = local_heads(queries, key_rows, value_rows, allowed)
    dec_own = swap_to_rows(dec_attended, 8).reshape(seq_rows, full_width)
    dec_mid = (embedded.astype(jnp.float32) + full_product(dec_own, dec_out)).astype(jnp.bfloat16)
    mid_normed = gather_rows(rms_norm(dec_mid, dec_norm2), 9)
    summed = feed_forward(mid_normed, dec_fc1, dec_fc2, 10)
    dec_final = (dec_mid.astype(jnp.float32) + summed).astype(jnp.bfloat16)
    next_normed = gather_rows(rms_norm(dec_final, next_norm), 11)
    next_local = dense(next_normed, next_qkv).astype(jnp.bfloat16)
    next_own = swap_to_rows(next_local, 12).reshape(seq_rows, gy_count, 3, local_width)
    return next_own.transpose(0, 2, 1, 3).reshape(seq_rows, 3, full_width)


def solution(mesh):
    placed = (
        P(("gx", "gy"), None),
        P(),
        P("gx"),
        P(),
        P(),
        P("gy", None),
        P(),
        P("gx", None, "gy"),
        P("gx", "gy"),
        P(),
        P("gx", "gy"),
        P("gx", "gy"),
        P(),
        P("gx", None, "gy"),
        P(),
        P("gx", None, "gy"),
        P("gx", "gy"),
        P(),
        P("gx", "gy"),
        P("gx", "gy"),
        P(),
        P("gx", None, "gy"),
    )
    return jax.shard_map(
        per_device,
        mesh=mesh,
        in_specs=placed,
        out_specs=P(("gx", "gy"), None, None),
        check_vma=False,
    )
```

```python
import jax
import jax.numpy as jnp
from jax import lax
from jax.experimental import pallas as pl
from jax.experimental.pallas import tpu as pltpu
from jax.sharding import PartitionSpec as P

HEAD_DIM = 88


norm_eps = 1e-06


def layer_norm(values, gain_row):
    values = values.astype(jnp.float32)
    centre = values - jnp.mean(values, axis=-1, keepdims=True)
    spread = jnp.mean(centre * centre, axis=-1, keepdims=True)
    return (centre * lax.rsqrt(spread + norm_eps) * gain_row).astype(jnp.bfloat16)


def rms_norm(values, gain_row):
    values = values.astype(jnp.float32)
    square = jnp.mean(values * values, axis=-1, keepdims=True)
    return (values * lax.rsqrt(square + norm_eps) * gain_row).astype(jnp.bfloat16)


def image_bounds(grid_rows):
    merged_count = grid_rows[:, 0] * grid_rows[:, 1]
    merged_end = jnp.cumsum(merged_count)
    return (merged_count, merged_end)


def patch_images(grid_rows, patch_slots):
    merged_count, merged_end = image_bounds(grid_rows)
    slot_index = jnp.arange(patch_slots, dtype=jnp.int32)
    return jnp.sum((slot_index[:, None] >= 4 * merged_end[None, :]).astype(jnp.int32), axis=1)


def merge_sources(grid_rows, merge_slots):
    image_count = grid_rows.shape[0]
    merged_count, merged_end = image_bounds(grid_rows)
    merged_start = merged_end - merged_count
    slot_index = jnp.arange(merge_slots, dtype=jnp.int32)
    image_of = jnp.sum((slot_index[:, None] >= merged_end[None, :]).astype(jnp.int32), axis=1)
    is_live = image_of < image_count
    picked = (
        jnp.minimum(image_of, image_count - 1)[:, None]
        == jnp.arange(image_count, dtype=jnp.int32)[None, :]
    ).astype(jnp.int32)
    col_count = jnp.sum(picked * grid_rows[None, :, 1], axis=1)
    first_slot = jnp.sum(picked * merged_start[None, :], axis=1)
    local_slot = slot_index - first_slot
    grid_row = local_slot // col_count
    grid_col = local_slot % col_count
    base_row = 4 * first_slot + 4 * grid_row * col_count + 2 * grid_col
    offsets = jnp.stack(
        [jnp.zeros_like(col_count), jnp.ones_like(col_count), 2 * col_count, 2 * col_count + 1],
        axis=1,
    )
    return jnp.where(is_live[:, None], base_row[:, None] + offsets, 0)


def request_of(index_rows, bounds):
    return jnp.sum((index_rows[:, None] >= bounds[None, :]).astype(jnp.int32), axis=1)


def local_heads(queries, key_rows, value_rows, allowed):
    scores = jnp.einsum(
        "qhe,khe->hqk", queries, key_rows, preferred_element_type=jnp.float32
    ) * HEAD_DIM ** (-0.5)
    exp_scores = jnp.where(allowed[None], jnp.exp(scores), 0.0)
    denominator = jnp.sum(exp_scores, axis=2)
    weighted = jnp.einsum(
        "hqk,khe->qhe",
        exp_scores.astype(jnp.bfloat16),
        value_rows,
        preferred_element_type=jnp.float32,
    )
    result = (weighted / denominator.T[:, :, None]).astype(jnp.bfloat16)
    return result.reshape(queries.shape[0], -1)


Z_COUNT = 4
MESH = pl.DeviceIdType.MESH


def grid_of(count):
    tall = Z_COUNT if count % Z_COUNT == 0 else 1
    return tall, count // tall


def column_parts(width, z_count, x_count):
    tiles = width // 128
    first = (tiles * 5 // 6 if 2 * x_count <= z_count else (tiles + 1) // 2) * 128
    return pl.ds(0, first), pl.ds(first, width - first)


def greet(places):
    barrier = pltpu.get_barrier_semaphore()
    for present, peer in places:
        @pl.when(present)
        def _():
            pl.semaphore_signal(barrier, inc=1, device_id={"gy": peer}, device_id_type=MESH)
    pl.semaphore_wait(barrier, sum(jnp.where(present, 1, 0) for present, peer in places))


def neighbours(z, x, z_count, x_count):
    return (
        (z > 0, jnp.maximum(z - 1, 0) * x_count + x),
        (z < z_count - 1, jnp.minimum(z + 1, z_count - 1) * x_count + x),
        (x > 0, z * x_count + jnp.maximum(x - 1, 0)),
        (x < x_count - 1, z * x_count + jnp.minimum(x + 1, x_count - 1)),
    )


def line_gather(count, pos, device_of, view, sends, recvs, enabled=None, arrived=None):
    last = count - 1
    sent = []
    for step in range(count - 1):
        moves = []
        for way in (0, 1):
            toward = 1 if way == 0 else -1
            own = pos - toward * step
            peer = pos + toward
            come = pos - toward * (step + 1)
            sending = (own >= 0) & (own <= last) & (peer >= 0) & (peer <= last)
            coming = (come >= 0) & (come <= last)
            if enabled is not None:
                sending, coming = sending & enabled, coming & enabled
            peer = jnp.clip(peer, 0, last)

            def copy_of(index, peer=peer, way=way, step=step):
                part = view(jnp.clip(index, 0, last))
                return pltpu.make_async_remote_copy(
                    src_ref=part,
                    dst_ref=part,
                    send_sem=sends(way, step),
                    recv_sem=recvs(way, step),
                    device_id={"gy": device_of(peer)},
                    device_id_type=MESH,
                )

            @pl.when(sending)
            def _():
                copy_of(own).start()

            moves.append((coming, come, copy_of, way))
            sent.append((sending, own, copy_of))
        yield
        for coming, come, copy_of, way in moves:
            @pl.when(coming)
            def _():
                copy_of(come).wait_recv()

            if arrived is not None:
                arrived(step, way, jnp.clip(come, 0, last), coming)
        yield
    for sending, own, copy_of in sent:
        @pl.when(sending)
        def _():
            copy_of(own).wait_send()


def chain(*lines):
    for line in lines:
        yield from line


def run_together(*lines):
    lines = list(lines)
    while lines:
        for line in list(lines):
            try:
                next(line)
            except StopIteration:
                lines.remove(line)


def gather_kernel(z_count, x_count, block, out, *sems):
    me = lax.axis_index("gy")
    z, x = me // x_count, me % x_count
    greet(neighbours(z, x, z_count, x_count))
    left, right = column_parts(block.shape[1], z_count, x_count)

    def along_z(k):
        return k * x_count + x

    def along_x(k):
        return z * x_count + k

    def pick(ref, *lead):
        return lambda way, step: ref.at[(*lead, way, step)]

    out[z, x] = block[...]

    def z_first():
        pending = []

        def onward(k, enabled, slot):
            line = line_gather(
                x_count, x, along_x, lambda q: out.at[k, q, :, left],
                pick(sems[2], slot), pick(sems[3], slot), enabled,
            )
            next(line, None)
            pending.append(line)

        onward(z, None, 0)
        yield from line_gather(
            z_count, z, along_z, lambda k: out.at[k, x, :, left], pick(sems[0]), pick(sems[1]),
            arrived=lambda step, way, k, coming: onward(k, coming, 1 + 2 * step + way),
        )
        for line in pending:
            yield from line

    run_together(
        z_first(),
        chain(
            line_gather(
                x_count, x, along_x, lambda k: out.at[z, k, :, right], pick(sems[4]), pick(sems[5])
            ),
            line_gather(
                z_count, z, along_z, lambda k: out.at[k, :, :, right], pick(sems[6]), pick(sems[7])
            ),
        ),
    )


def line_reduce(count, pos, device_of, own, store, outgoing, incoming, sends, recvs):
    last = count - 1

    def copy_of(way, slot):
        return pltpu.make_async_remote_copy(
            src_ref=outgoing.at[way, slot],
            dst_ref=incoming.at[way, slot],
            send_sem=sends.at[way, slot],
            recv_sem=recvs.at[way, slot],
            device_id={"gy": device_of(jnp.clip(pos + (1 if way == 0 else -1), 0, last))},
            device_id_type=MESH,
        )

    behind = (pos, last - pos)
    for time in range(count - 1):
        for way in (0, 1):
            slot = jnp.clip(time - behind[way], 0, last - 1)
            dest = last - slot if way == 0 else slot

            @pl.when((behind[way] > 0) & (behind[way] <= time))
            def _():
                copy_of(way, slot).wait_recv()
                outgoing[way, slot] = (
                    own(dest) + incoming[way, slot].astype(jnp.float32)
                ).astype(jnp.bfloat16)
                copy_of(way, slot).start()

            @pl.when(behind[way] == 0)
            def _():
                outgoing[way, slot] = own(dest).astype(jnp.bfloat16)
                copy_of(way, slot).start()

        yield
    store(own(pos))
    yield
    for way in (0, 1):
        @pl.when(behind[way] > 0)
        def _():
            slot = jnp.clip(last - behind[way], 0, max(last - 1, 0))
            copy_of(way, slot).wait_recv()
            store(None, incoming[way, slot].astype(jnp.float32))
    for time in range(count - 1):
        for way in (0, 1):
            @pl.when(behind[way] <= time)
            def _():
                copy_of(way, jnp.clip(time - behind[way], 0, last - 1)).wait_send()


def reduce_kernel(z_count, x_count, terms, out, sum_l, sum_r, total_l, total_r, *rest):
    bufs, sems = rest[:8], rest[8:]
    me = lax.axis_index("gy")
    z, x = me // x_count, me % x_count
    greet(neighbours(z, x, z_count, x_count))
    left, right = column_parts(terms.shape[3], z_count, x_count)

    def along_z(k):
        return k * x_count + x

    def along_x(k):
        return z * x_count + k

    def keep(ref):
        def store(first, more=None):
            if more is None:
                ref[...] = first
            else:
                ref[...] += more

        return store

    run_together(
        chain(
            line_reduce(
                x_count, x, along_x, lambda k: terms[:, k, :, left].astype(jnp.float32),
                keep(sum_l), bufs[0], bufs[1], sems[0], sems[1],
            ),
            line_reduce(
                z_count, z, along_z, lambda k: sum_l[k], keep(total_l),
                bufs[2], bufs[3], sems[2], sems[3],
            ),
        ),
        chain(
            line_reduce(
                z_count, z, along_z, lambda k: terms[k, :, :, right].astype(jnp.float32),
                keep(sum_r), bufs[4], bufs[5], sems[4], sems[5],
            ),
            line_reduce(
                x_count, x, along_x, lambda k: sum_r[k], keep(total_r),
                bufs[6], bufs[7], sems[6], sems[7],
            ),
        ),
    )
    out[:, left] = total_l[...]
    out[:, right] = total_r[...]


def swap_kernel(count, blocks, out, sends, recvs):
    me = lax.axis_index("gy")
    barrier = pltpu.get_barrier_semaphore()
    for shift in range(1, count):
        peer = lax.rem(me + shift, count)
        pl.semaphore_signal(barrier, inc=1, device_id={"gy": peer}, device_id_type=MESH)
    pl.semaphore_wait(barrier, count - 1)
    copies = []
    for shift in range(1, count):
        peer = lax.rem(me + shift, count)
        copy = pltpu.make_async_remote_copy(
            src_ref=blocks.at[peer],
            dst_ref=out.at[me],
            send_sem=sends.at[shift - 1],
            recv_sem=recvs.at[shift - 1],
            device_id={"gy": peer},
            device_id_type=MESH,
        )
        copy.start()
        copies.append(copy)
    out[me] = blocks[me]
    for copy in copies:
        copy.wait_recv()
    for copy in copies:
        copy.wait_send()


def call(body, out_shape, scratch, identity, name, size):
    whole = pl.BlockSpec(memory_space=pltpu.VMEM)
    return pl.pallas_call(
        body,
        out_shape=out_shape,
        in_specs=[whole],
        out_specs=whole,
        scratch_shapes=scratch,
        name=name,
        cost_estimate=pl.CostEstimate(flops=0, bytes_accessed=size, transcendentals=0),
        compiler_params=pltpu.CompilerParams(
            collective_id=identity, has_side_effects=True, vmem_limit_bytes=48 * 1024 * 1024
        ),
    )


def pair(count, *lead):
    sems = pltpu.SemaphoreType.DMA((*lead, 2, max(count - 1, 1)))
    return [sems, sems]


def gather_rows(block, identity):
    z_count, x_count = grid_of(lax.axis_size("gy"))
    rows, width = block.shape
    scratch = pair(z_count) + pair(x_count, 2 * z_count - 1) + pair(x_count) + pair(z_count)
    out = call(
        lambda *refs: gather_kernel(z_count, x_count, *refs),
        jax.ShapeDtypeStruct((z_count, x_count, rows, width), jnp.bfloat16),
        scratch, identity, "gather_rows", 60000000,
    )(block)
    return out.reshape(z_count * x_count * rows, width)


def sum_rows(terms, identity):
    z_count, x_count = grid_of(lax.axis_size("gy"))
    width = terms.shape[1]
    rows = terms.shape[0] // (z_count * x_count)
    left, right = column_parts(width, z_count, x_count)
    l_size, r_size = left.size, right.size

    def slots(count, *shape):
        slot = pltpu.VMEM((2, max(count - 1, 1)) + shape, jnp.bfloat16)
        return [slot, slot]

    scratch = (
        [
            pltpu.VMEM((z_count, rows, l_size), jnp.float32),
            pltpu.VMEM((x_count, rows, r_size), jnp.float32),
            pltpu.VMEM((rows, l_size), jnp.float32),
            pltpu.VMEM((rows, r_size), jnp.float32),
        ]
        + slots(x_count, z_count, rows, l_size)
        + slots(z_count, rows, l_size)
        + slots(z_count, x_count, rows, r_size)
        + slots(x_count, rows, r_size)
        + pair(x_count) + pair(z_count) + pair(z_count) + pair(x_count)
    )
    return call(
        lambda *refs: reduce_kernel(z_count, x_count, *refs),
        jax.ShapeDtypeStruct((rows, width), jnp.float32),
        scratch, identity, "sum_rows", 60000000,
    )(terms.reshape(z_count, x_count, rows, width))


def swap_to_rows(values, identity):
    count = lax.axis_size("gy")
    rows, width = values.shape[0] // count, values.shape[1]
    sems = pltpu.SemaphoreType.DMA((count - 1,))
    out = call(
        lambda *refs: swap_kernel(count, *refs),
        jax.ShapeDtypeStruct((count, rows, width), jnp.bfloat16),
        [sems, sems], identity, "swap_to_rows", 20000000,
    )(values.reshape(count, rows, width))
    return out.transpose(1, 0, 2)


def full_weight(weight):
    return lax.all_gather(weight, ("gx", "gy"), axis=0, tiled=False)


def full_product(rows, blocks):
    gx_count, gy_count = lax.axis_size("gx"), lax.axis_size("gy")
    depth, width = blocks.shape[1:]
    total = jnp.zeros((gy_count, rows.shape[0], width), jnp.float32)
    for i in range(gx_count):
        part = rows[:, i * depth : (i + 1) * depth]
        total = total + jnp.einsum(
            "jtk,jkn->jtn",
            jnp.broadcast_to(part[None], (gy_count,) + part.shape),
            blocks[i * gy_count : (i + 1) * gy_count],
            preferred_element_type=jnp.float32,
        )
    return total.transpose(1, 0, 2).reshape(rows.shape[0], gy_count * width)


def weight_columns(weight):
    return lax.all_gather(weight.reshape(weight.shape[0], -1), "gx", axis=0, tiled=True)


def dense(rows, weight):
    return jnp.dot(rows, weight, preferred_element_type=jnp.float32)


def feed_forward(normed_full, fc_in, fc_back, identity):
    hidden = jax.nn.gelu(dense(normed_full, fc_in), approximate=False).astype(jnp.bfloat16)
    partial_sum = lax.dot_general(
        hidden, fc_back, (((1,), (1,)), ((), ())), preferred_element_type=jnp.float32
    )
    return sum_rows(partial_sum.astype(jnp.bfloat16), identity)


def per_device(
    patches,
    grids,
    text_ids,
    positions,
    lengths,
    text_table,
    vit_norm1,
    vit_qkv,
    vit_out,
    vit_norm2,
    vit_fc1,
    vit_fc2,
    merge_norm,
    merge_proj,
    dec_norm1,
    dec_qkv,
    dec_out,
    dec_norm2,
    dec_fc1,
    dec_fc2,
    next_norm,
    next_qkv,
):
    gx_count = lax.axis_size("gx")
    gx_index = lax.axis_index("gx")
    gy_count = lax.axis_size("gy")
    gy_index = lax.axis_index("gy")
    per_group = grids.shape[0] // gx_count
    own_grids = lax.dynamic_slice_in_dim(grids, gx_index * per_group, per_group, 0)
    local_width = vit_qkv.shape[2]
    head_count = local_width // HEAD_DIM
    vit_qkv, vit_fc1, vit_fc2, merge_proj = [
        weight_columns(weight) for weight in (vit_qkv, vit_fc1, vit_fc2, merge_proj)
    ]
    vit_out = full_weight(vit_out)

    patches_full = gather_rows(patches, 0)
    patch_slots, full_width = patches_full.shape
    merge_slots = positions.shape[0] // gx_count
    sources = merge_sources(own_grids, merge_slots).reshape(merge_slots * 4)
    slot_index = jnp.arange(patch_slots, dtype=jnp.int32)
    chosen = (sources[:, None] == slot_index[None, :]).astype(jnp.bfloat16)
    ordered = dense(chosen, patches_full).astype(jnp.bfloat16)
    triple = dense(layer_norm(ordered, vit_norm1), vit_qkv).astype(jnp.bfloat16)
    triple = triple.reshape(patch_slots, 3, head_count, HEAD_DIM)
    image_ids = jnp.sum(
        (sources[:, None] >= 4 * image_bounds(own_grids)[1][None, :]).astype(jnp.int32), axis=1
    )
    is_key = slot_index < 4 * jnp.sum(own_grids[:, 0] * own_grids[:, 1])
    attended = local_heads(
        triple[:, 0],
        triple[:, 1],
        triple[:, 2],
        (image_ids[:, None] == image_ids[None, :]) & is_key[None, :],
    )
    attended, dec_qkv, dec_out, dec_fc1, dec_fc2 = lax.optimization_barrier(
        (attended, dec_qkv, dec_out, dec_fc1, dec_fc2)
    )
    dec_qkv, dec_fc1, dec_fc2 = [
        weight_columns(weight) for weight in (dec_qkv, dec_fc1, dec_fc2)
    ]
    dec_out = full_weight(dec_out)
    own_rows = patch_slots // gy_count
    patches_own = lax.dynamic_slice_in_dim(ordered, gy_index * own_rows, own_rows, 0)
    attended_own = swap_to_rows(attended, 1).reshape(own_rows, full_width)
    vit_mid = (patches_own.astype(jnp.float32) + full_product(attended_own, vit_out)).astype(jnp.bfloat16)
    vit_normed = gather_rows(layer_norm(vit_mid, vit_norm2), 2)
    summed = feed_forward(vit_normed, vit_fc1, vit_fc2, 3)
    vit_final = (vit_mid.astype(jnp.float32) + summed).astype(jnp.bfloat16)
    merged = vit_final.astype(jnp.float32).reshape(own_rows // 4, 4, full_width)
    centre = merged - jnp.mean(merged, axis=(1, 2), keepdims=True)
    spread = jnp.mean(centre * centre, axis=(1, 2), keepdims=True)
    merged_normed = (centre * lax.rsqrt(spread + norm_eps) * merge_norm).astype(jnp.bfloat16)
    merged_full = gather_rows(merged_normed.reshape(own_rows, full_width), 4)
    products = dense(merged_full, merge_proj).reshape(merge_slots, 4, 4 * local_width)
    projected = products[:, 0, :local_width]
    for k in range(1, 4):
        projected = projected + products[:, k, k * local_width : (k + 1) * local_width]
    projected = projected.astype(jnp.bfloat16)

    seq_slots = text_ids.shape[0]
    seq_rows = seq_slots // gy_count
    seq_index = gx_index * seq_slots + jnp.arange(seq_slots, dtype=jnp.int32)
    matches = positions[None, :] == seq_index[:, None]
    all_projected = lax.all_gather(projected, "gx", axis=0, tiled=True)
    placed = dense(matches.astype(jnp.bfloat16), all_projected).astype(jnp.bfloat16)
    placed_own = swap_to_rows(placed, 5).reshape(seq_rows, full_width)
    vocab_rows = text_table.shape[0]
    shifted_ids = text_ids - gy_index * vocab_rows
    inside = (shifted_ids >= 0) & (shifted_ids < vocab_rows)
    looked_up = jnp.take(text_table, jnp.clip(shifted_ids, 0, vocab_rows - 1), axis=0)
    table_terms = jnp.where(inside[:, None], looked_up, jnp.bfloat16(0))
    text_own = sum_rows(table_terms, 6).astype(jnp.bfloat16)
    is_image = lax.dynamic_slice_in_dim(
        jnp.any(matches, axis=1), gy_index * seq_rows, seq_rows, 0
    )
    embedded = jnp.where(is_image[:, None], placed_own, text_own)

    dec_normed = gather_rows(rms_norm(embedded, dec_norm1), 7)
    dec_triple = dense(dec_normed, dec_qkv).astype(jnp.bfloat16)
    bounds = jnp.cumsum(lengths)
    own_request = request_of(seq_index, bounds)
    dec_triple = dec_triple.reshape(seq_slots, 3, local_width)
    key_rows = lax.all_gather(dec_triple[:, 1], "gx", axis=0, tiled=True)
    value_rows = lax.all_gather(dec_triple[:, 2], "gx", axis=0, tiled=True)
    key_count = key_rows.shape[0]
    key_rows = key_rows.reshape(key_count, head_count, HEAD_DIM)
    value_rows = value_rows.reshape(key_count, head_count, HEAD_DIM)
    key_index = jnp.arange(key_count, dtype=jnp.int32)
    allowed = (request_of(key_index, bounds)[None, :] == own_request[:, None]) & (
        key_index[None, :] <= seq_index[:, None]
    )
    queries = dec_triple[:, 0].reshape(seq_slots, head_count, HEAD_DIM)
    dec_attended = local_heads(queries, key_rows, value_rows, allowed)
    dec_own = swap_to_rows(dec_attended, 8).reshape(seq_rows, full_width)
    dec_mid = (embedded.astype(jnp.float32) + full_product(dec_own, dec_out)).astype(jnp.bfloat16)
    dec_mid, next_qkv = lax.optimization_barrier((dec_mid, next_qkv))
    next_qkv = weight_columns(next_qkv)
    mid_normed = gather_rows(rms_norm(dec_mid, dec_norm2), 9)
    summed = feed_forward(mid_normed, dec_fc1, dec_fc2, 10)
    dec_final = (dec_mid.astype(jnp.float32) + summed).astype(jnp.bfloat16)
    next_normed = gather_rows(rms_norm(dec_final, next_norm), 11)
    next_local = dense(next_normed, next_qkv).astype(jnp.bfloat16)
    next_own = swap_to_rows(next_local, 12).reshape(seq_rows, gy_count, 3, local_width)
    return next_own.transpose(0, 2, 1, 3).reshape(seq_rows, 3, full_width)


def solution(mesh):
    placed = (
        P(("gx", "gy"), None),
        P(),
        P("gx"),
        P(),
        P(),
        P("gy", None),
        P(),
        P("gx", None, "gy"),
        P("gx", "gy"),
        P(),
        P("gx", "gy"),
        P("gx", "gy"),
        P(),
        P("gx", None, "gy"),
        P(),
        P("gx", None, "gy"),
        P("gx", "gy"),
        P(),
        P("gx", "gy"),
        P("gx", "gy"),
        P(),
        P("gx", None, "gy"),
    )
    return jax.shard_map(
        per_device,
        mesh=mesh,
        in_specs=placed,
        out_specs=P(("gx", "gy"), None, None),
        check_vma=False,
    )
```
